512 devices in a mesh: dp: 64 (over y, x, z_hi, core), frame: 8 (over z_lo).
Axes of the slice: x: 4, y: 4, z: 16 (z_hi: 2, z_lo: 8; z = z_hi * 8 + z_lo), core: 2. Of those that a mesh axis runs over, the one named last changes fastest.
Arguments:
- video_tokens: bfloat16 [1024, 8, 32, 1024], P('dp', 'frame'), may hold values from -14 to 14
- pool_weight: bfloat16 [8, 16, 32], P('frame'), may hold values from -1 to 1
- text_states: bfloat16 [1024, 77, 1600], P(('dp', 'frame')), may hold values from -6 to 6
- norm_gain: float32 [1600], replicated, may hold values from 0.5 to 1.5
- lengths: int32 [1024], P(('dp', 'frame')), may hold values from 1 to 77
- cotangent: bfloat16 [1024, 77, 1600], P(('dp', 'frame')), may hold values from -6 to 6
- query_weight: bfloat16 [1600, 896], P('dp'), may hold values from -0.15625 to 0.15625
- key_weight: bfloat16 [1024, 896], P('dp'), may hold values from -0.1875 to 0.1875
- value_weight: bfloat16 [1024, 896], P('dp'), may hold values from -0.1875 to 0.1875
- out_weight: bfloat16 [896, 1600], P('dp'), may hold values from -0.1875 to 0.1875
Outputs:
- grad_text: bfloat16 [1024, 77, 1600], P(('dp', 'frame'))
- grad_pooled: bfloat16 [1024, 128, 1024], P('dp', 'frame')
The draws below stay inside these ranges and needn't reach their ends.
Inputs may be any that keep to these rules, and one draw needn't show every extreme that they name: `lengths`: text positions at or after a clip's length are padding.
All inputs are finite; a program needn't handle non-finite values.
Results may differ from the reference program's by a relative error of at most 0.02.
The reference program's roundings to bfloat16 on the way count: a program that leaves them out, or rounds other values in their place, can miss the bound.
Values may be sent and summed in bfloat16 or wider, within the bound.
A program may use at most 64 MiB of HBM per device.

```python
import jax
import jax.numpy as jnp
from jax import lax

D = 1600
V = 1024
HEADS = 14
HD = 64
TEXT = 77
PATCH = 32
LAT_F = 16
CLIP_DEV = 16
HW = 896
FRAMES = 8
LATENTS = 128
CLIPS = 1024


def draw_video_tokens(key, part):
    array_shape = (CLIPS, FRAMES, PATCH, V)
    result = jnp.clip(jax.random.normal(key, array_shape, jnp.float32), -6.0, 6.0)
    return result.astype(jnp.bfloat16)


def place_ends(values, stream_key, low, high):
    extent = values.shape
    spot = [jax.random.randint(jax.random.fold_in(stream_key, axis), (), 0, extent[axis]) for axis in range(len(extent))]
    values = values.at[tuple(spot)].set(low)
    longest = extent.index(max(extent))
    spot[longest] = (spot[longest] + 1) % extent[longest]
    return values.at[tuple(spot)].set(high)


def levels(key, shape, cuts, least, high):
    level = 1.0
    for dim, shards_of in cuts:
        draws = jax.random.uniform(jax.random.fold_in(jax.random.fold_in(key, 6), dim), (shards_of,), jnp.float32, least / len(cuts), high / len(cuts))
        level = level * jnp.repeat(jnp.exp(draws), shape[dim] // shards_of).reshape((-1,) + (1,) * (len(shape) - 1 - dim))
    return level


def centred(rng, shape, scale, most, shards=(), held_as=jnp.bfloat16):
    loudness = levels(rng, shape, shards, -0.22, 0.18) if shards else 1.0
    values = jax.random.normal(rng, shape, jnp.float32) * scale * loudness
    return jnp.minimum(jnp.maximum(values, -most), most).astype(held_as)


def setup_inputs(seed: int = 0) -> dict:
    splits = jax.random.split(jax.random.key(seed), 11)
    return {
        "video_tokens": draw_video_tokens(jax.random.fold_in(splits[10], 71), 0),
        "pool_weight": centred(splits[1], (FRAMES, LAT_F, PATCH), PATCH ** -0.5, 1.0, ((0, 8),)),
        "text_states": centred(splits[2], (CLIPS, TEXT, D), 1.0, 6.0, ((0, 512),)),
        "norm_gain": jnp.clip(1.0 + 0.1 * jax.random.normal(splits[3], (D,), jnp.float32), 0.5, 1.5),
        "lengths": place_ends(jax.random.randint(splits[4], (CLIPS,), 1, TEXT + 1), jax.random.fold_in(splits[4], 1), 1, TEXT).astype(jnp.int32),
        "cotangent": centred(splits[5], (CLIPS, TEXT, D), 1.0, 6.0, ((0, 512),)),
        "query_weight": centred(splits[6], (D, HW), D ** -0.5, 0.15625, ((0, 64),)),
        "key_weight": centred(splits[7], (V, HW), V ** -0.5, 0.1875, ((0, 64),)),
        "value_weight": centred(splits[8], (V, HW), V ** -0.5, 0.1875, ((0, 64),)),
        "out_weight": centred(splits[9], (HW, D), HW ** -0.5, 0.1875, ((0, 64),)),
    }


EPSILON = 1e-05

def product(left, right):
    return jnp.dot(left, right, preferred_element_type=jnp.float32)

def product_back(left, right):
    return lax.dot_general(left, right, (((1,), (1,)), ((), ())), preferred_element_type=jnp.float32)

def rounded(array):
    return lax.optimization_barrier(array.astype(jnp.bfloat16))

def split_heads(array, clip_count):
    return array.reshape(clip_count, -1, HEADS, HD).astype(jnp.float32)

def one_block(video_tokens, pool_weight, text_states, norm_gain, lengths, cotangent, query_weight, key_weight, value_weight, out_weight):
    clip_count = video_tokens.shape[0]
    highest = lax.Precision.HIGHEST
    score_scale = HD ** (-0.5)
    pooled = jnp.einsum('flp,cfpv->cflv', pool_weight.astype(jnp.float32), video_tokens.astype(jnp.float32), precision=highest)
    pooled = rounded(pooled).reshape(clip_count * LATENTS, V)
    key_rows = rounded(product(pooled, key_weight))
    value_rows = rounded(product(pooled, value_weight))
    text_rows = text_states.reshape(clip_count * TEXT, D).astype(jnp.float32)
    average = lax.optimization_barrier(jnp.mean(text_rows, axis=1, keepdims=True))
    centered = text_rows - average
    inverse = lax.rsqrt(lax.optimization_barrier(jnp.mean(centered * centered, axis=1, keepdims=True)) + EPSILON)
    unit_rows = centered * inverse
    normed = rounded(unit_rows * norm_gain)
    queries = rounded(product(normed, query_weight))
    query_heads = split_heads(queries, clip_count)
    key_heads = split_heads(key_rows, clip_count)
    value_heads = split_heads(value_rows, clip_count)
    scores = jnp.einsum('cthd,clhd->chtl', query_heads, key_heads, precision=highest) * score_scale
    row_max = lax.optimization_barrier(jnp.max(scores, axis=3, keepdims=True))
    shifted = jnp.exp(scores - row_max)
    attn_probs = shifted / lax.optimization_barrier(jnp.sum(shifted, axis=3, keepdims=True))
    probs_low = rounded(attn_probs).astype(jnp.float32)
    attended = rounded(jnp.einsum('chtl,clhd->cthd', probs_low, value_heads, precision=highest)).astype(jnp.float32)
    positions = jnp.arange(TEXT, dtype=jnp.int32)
    valid_mask = positions[None, :] < lengths[:, None]
    grad_out = jnp.where(valid_mask[:, :, None], cotangent, jnp.zeros_like(cotangent)).reshape(clip_count * TEXT, D)
    grad_att = rounded(product_back(grad_out, out_weight))
    grad_heads = split_heads(grad_att, clip_count)
    grad_probs = jnp.einsum('cthd,clhd->chtl', grad_heads, value_heads, precision=highest)
    row_term = jnp.einsum('cthd,cthd->cht', grad_heads, attended, precision=highest)[..., None]
    grad_scores = rounded(attn_probs * (grad_probs - row_term) * score_scale).astype(jnp.float32)
    grad_queries = rounded(jnp.einsum('chtl,clhd->cthd', grad_scores, key_heads, precision=highest)).reshape(clip_count * TEXT, HW)
    grad_keys = rounded(jnp.einsum('chtl,cthd->clhd', grad_scores, query_heads, precision=highest)).reshape(clip_count * LATENTS, HW)
    grad_values = rounded(jnp.einsum('chtl,cthd->clhd', probs_low, grad_heads, precision=highest)).reshape(clip_count * LATENTS, HW)
    grad_pooled = (product_back(grad_keys, key_weight) + product_back(grad_values, value_weight)).astype(jnp.bfloat16)
    grad_normed = product_back(grad_queries, query_weight)
    scaled_grad = grad_normed * norm_gain
    grad_rows = inverse * (scaled_grad - lax.optimization_barrier(jnp.mean(scaled_grad, axis=1, keepdims=True)) - unit_rows * lax.optimization_barrier(jnp.mean(scaled_grad * unit_rows, axis=1, keepdims=True)))
    return (grad_rows.astype(jnp.bfloat16).reshape(clip_count, TEXT, D), grad_pooled.reshape(clip_count, LATENTS, V))

def reference(video_tokens, pool_weight, text_states, norm_gain, lengths, cotangent, query_weight, key_weight, value_weight, out_weight):
    blocks = CLIPS // CLIP_DEV

    def process(pieces):
        return one_block(pieces[0], pool_weight, pieces[1], norm_gain, pieces[2], pieces[3], query_weight, key_weight, value_weight, out_weight)
    shaped = (video_tokens.reshape(blocks, CLIP_DEV, FRAMES, PATCH, V), text_states.reshape(blocks, CLIP_DEV, TEXT, D), lengths.reshape(blocks, CLIP_DEV), cotangent.reshape(blocks, CLIP_DEV, TEXT, D))
    grad_text, grad_pooled = lax.map(process, shaped)
    return (grad_text.reshape(CLIPS, TEXT, D), grad_pooled.reshape(CLIPS, LATENTS, V))
```

```python
import functools

import jax
import jax.numpy as jnp
from jax import lax
from jax.experimental import pallas as pl
from jax.experimental.pallas import tpu as pltpu
from jax.sharding import PartitionSpec as P

HD = 64
EPSILON = 1e-05
MESH = pl.DeviceIdType.MESH
F32 = jnp.float32
BF16 = jnp.bfloat16

D = 1600
DP = 1664
V = 1024
HW = 896
TEXT = 77
TP = 80
QL = 1408
LAT = 16
FRAMES = 8
ROWS = 2 * TP


def dot(left, right):
    return jnp.dot(left, right, preferred_element_type=F32)


def dot_nt(left, right):
    return lax.dot_general(left, right, (((1,), (1,)), ((), ())), preferred_element_type=F32)


def dot_tn(left, right):
    return lax.dot_general(left, right, (((0,), (0,)), ((), ())), preferred_element_type=F32)


def kernel(
    video, pool_w, text, gain_in, lengths, cot, q_in, k_in, v_in, o_in,
    grad_text, grad_pooled,
    qb, ob, kb, vb, qw, ow, qf, of, qs, os_, xs, cs, gain, unit, normed, go, queries, ga,
    pooled, lat, kl, vl, gk, gv, gq, back,
    send, recv, cross_send, cross_recv, pool_send, pool_recv, back_send, back_recv, own_sem,
):
    dp = lax.axis_index("dp")
    f = lax.axis_index("frame")
    y, x, h, c = dp // 16, (dp // 4) % 4, (dp // 2) % 2, dp % 2
    o = 1 - h

    def device(y, x, h, c, f):
        return (((y * 4 + x) * 2 + h) * 2 + c, f)

    def up(i):
        return (i + 1) % 4

    def down(i):
        return (i + 3) % 4

    def far(i):
        return (i + 2) % 4

    sibling = device(y, x, h, 1 - c, f)
    x_up, x_down = device(y, up(x), h, c, f), device(y, down(x), h, c, f)
    y_up, y_down = device(up(y), x, h, c, f), device(down(y), x, h, c, f)

    barrier = pltpu.get_barrier_semaphore()

    def greet(who):
        pl.semaphore_signal(barrier, inc=1, device_id=who, device_id_type=MESH)

    for who in (sibling, x_up, x_down, y_up, y_down):
        greet(who)
    for step in range(1, FRAMES):
        greet((dp, (f + step) % FRAMES))
    other_dp = device(y, x, o, c, f)[0]
    at_low = f == 0
    at_high = f == FRAMES - 1
    at_end = jnp.logical_or(at_low, at_high)

    @pl.when(at_low)
    def _():
        for k in range(4):
            greet((other_dp, 7 - k))

    @pl.when(at_high)
    def _():
        for k in range(4):
            greet((other_dp, k))

    @pl.when(jnp.logical_not(at_end))
    def _():
        greet((other_dp, jnp.where(f < 4, FRAMES - 1, 0)))

    qs[...] = jnp.zeros_like(qs)
    q = q_in[...].astype(F32)
    qs[:, 0:HW] = q[0:16]
    qs[0:8, HW:QL] = q[16:24, 0:512]
    qs[8:16, HW:HW + 384] = q[16:24, 512:HW]
    for b in range(7):
        qs[8 + b:9 + b, HW + 384:QL] = q[24:25, 128 * b:128 * b + 128]
    qb[y, x, h, c] = qs[...].astype(BF16)
    os_[...] = jnp.zeros_like(os_)
    os_[0:14, 0:D] = o_in[...].astype(F32)
    ob[y, x, h, c] = os_[...].astype(BF16)
    kb[y, x, h, c] = k_in[...]
    vb[y, x, h, c] = v_in[...]

    i0 = lax.broadcasted_iota(jnp.int32, (32, 256), 0)
    i1 = lax.broadcasted_iota(jnp.int32, (32, 256), 1)
    spread = jnp.where(i1 % 32 == i0, 1.0, 0.0).astype(BF16)
    wide = dot(pool_w[...], spread)
    wide = jnp.concatenate([wide] * 8, axis=0)
    j0 = lax.broadcasted_iota(jnp.int32, (128, 256), 0)
    j1 = lax.broadcasted_iota(jnp.int32, (128, 256), 1)
    diag = jnp.where(j0 // 16 == j1 // 32, wide, 0.0).astype(BF16)
    for half in range(2):
        part = dot(diag, video[256 * half:256 * half + 256, :])
        pooled[128 * half:128 * half + 128, :] = part.astype(BF16)

    count = 12 + jnp.where(at_end, 4, 1)
    pl.semaphore_wait(barrier, count)

    bufs = (qb, ob, kb, vb)
    x_first = (True, False, True, False)
    sends = []

    def copy(src, dst, s_sem, r_sem, who):
        return pltpu.make_async_remote_copy(
            src_ref=src, dst_ref=dst, send_sem=s_sem, recv_sem=r_sem, device_id=who,
            device_id_type=MESH)

    def parts(w):
        buf = bufs[w]
        if x_first[w]:
            return (
                lambda a, z: buf.at[y, a, z, c],
                lambda b, z: buf.at[b, :, z, c],
                lambda b, z, k: buf.at[b, pl.ds(2 * k, 2), z, c],
                (lambda b, z: buf.at[b, :, z, 1 - c]),
                x, y, x_up, x_down, y_up, y_down,
            )
        return (
            lambda a, z: buf.at[a, x, z, c],
            lambda b, z: buf.at[:, b, z, c],
            lambda b, z, k: buf.at[pl.ds(2 * k, 2), b, z, c],
            (lambda b, z: buf.at[:, b, z, 1 - c]),
            y, x, y_up, y_down, x_up, x_down,
        )

    def step(w, s, k):
        item, row, pair, other_row, a, b, a_up, a_down, b_up, b_down = parts(w)
        z = h if s == 0 else o

        def go_(ref, index, who):
            moving = copy(ref, ref, send.at[w, s, index], recv.at[w, s, index], who)
            moving.start()
            sends.append(moving)

        def come(ref, index, who):
            copy(ref, ref, send.at[w, s, index], recv.at[w, s, index], who).wait_recv()

        if k == 0:
            if s == 1:
                mine = bufs[w].at[y, x, o, c]
                copy(mine, mine, cross_send.at[w, 0], cross_recv.at[w], (other_dp, f)).wait_recv()
            go_(item(a, z), 0, a_up)
            go_(item(a, z), 1, a_down)
        elif k == 1:
            if s == 0:
                come(item(down(a), z), 0, a_up)
                go_(item(down(a), z), 2, a_up)
                come(item(up(a), z), 1, a_down)
            else:
                come(item(up(a), z), 1, a_down)
                go_(item(up(a), z), 2, a_down)
                come(item(down(a), z), 0, a_up)
        elif k == 2:
            come(item(far(a), z), 2, a_up if s == 0 else a_down)
            go_(pair(b, z, 0), 3, b_up)
            go_(pair(b, z, 1), 6, b_down)
            go_(pair(b, z, 1), 4, b_up)
            go_(pair(b, z, 0), 5, b_down)
            go_(row(b, z), 9, sibling)
        elif k == 3:
            come(pair(down(b), z, 0), 3, b_up)
            go_(pair(down(b), z, 0), 7, b_up)
            come(pair(up(b), z, 1), 6, b_down)
            go_(pair(up(b), z, 1), 8, b_down)
            come(pair(down(b), z, 1), 4, b_up)
            go_(row(down(b), z), 10, sibling)
            come(pair(up(b), z, 0), 5, b_down)
            go_(row(up(b), z), 11, sibling)
        elif k == 4:
            come(pair(far(b), z, 0), 7, b_up)
            come(pair(far(b), z, 1), 8, b_down)
            go_(row(far(b), z), 12, sibling)
        else:
            for n, at in enumerate((b, down(b), up(b), far(b))):
                ref = other_row(at, z)
                copy(ref, ref, send.at[w, s, 9 + n], recv.at[w, s, 9 + n], sibling).wait_recv()

    units = ((0, 1, 0), (0, 1, 1), (2, 3, 0), (2, 3, 1))

    def round_(r):
        for u, (w0, w1, s) in enumerate(units):
            k = r - u
            if 0 <= k <= 4:
                step(w0, s, k)
                step(w1, s, k)

    round_(0)

    def cross(where, k, w, target):
        mine = bufs[w].at[y, x, h, c]
        return copy(mine, mine, cross_send.at[w, k], cross_recv.at[w], (other_dp, target))

    @pl.when(at_low)
    def _():
        for w in range(4):
            for k in range(4):
                cross(0, k, w, 4 + k).start()

    @pl.when(at_high)
    def _():
        for w in range(4):
            for k in range(4):
                cross(1, k, w, 3 - k).start()

    def pool_copy(clip, to, frm):
        start = pl.multiple_of(32 * to + 16 * clip, 16)
        place = pl.multiple_of(16 * frm, 16)
        return copy(
            pooled.at[pl.ds(start, 16), :], lat.at[clip, pl.ds(place, 16), :],
            pool_send.at[clip, to], pool_recv.at[clip, frm], (dp, to))

    for clip in range(2):
        for n in range(1, FRAMES):
            pool_copy(clip, (f + n) % FRAMES, f).start()
        start = pl.multiple_of(32 * f + 16 * clip, 16)
        place = pl.multiple_of(16 * f, 16)
        lat[clip, pl.ds(place, 16), :] = pooled[pl.ds(start, 16), :]

    gain[...] = jnp.zeros_like(gain)
    gain[0:1, 0:D] = gain_in[...]
    xs[...] = jnp.zeros_like(xs)
    cs[...] = jnp.zeros_like(cs)
    for clip in range(2):
        xs[TP * clip:TP * clip + TEXT, 0:D] = text[clip].astype(F32)
        cs[TP * clip:TP * clip + TEXT, 0:D] = cot[clip].astype(F32)
    round_(1)
    lane = lax.broadcasted_iota(jnp.int32, (TP, DP), 1)
    position = lax.broadcasted_iota(jnp.int32, (TP, DP), 0)
    inverses = []
    for clip in range(2):
        rows = slice(TP * clip, TP * clip + TP)
        states = xs[rows, :]
        average = jnp.sum(states, axis=1, keepdims=True) * (1.0 / D)
        centered = jnp.where(lane < D, states - average, 0.0)
        square = jnp.sum(centered * centered, axis=1, keepdims=True) * (1.0 / D)
        inverse = lax.rsqrt(square + EPSILON)
        inverses.append(inverse)
        unit_rows = centered * inverse
        unit[rows, :] = unit_rows
        normed[rows, :] = (unit_rows * gain[0:1, :]).astype(BF16)
        go[rows, :] = jnp.where(position < lengths[clip], cs[rows, :], 0.0).astype(BF16)
    round_(2)
    round_(3)
    round_(4)
    round_(5)

    qw[D:DP, :] = jnp.zeros((DP - D, HW), BF16)
    for s in range(2):
        for w in range(2):
            step(w, s, 5)

    def unpack(j, carry):
        for k in range(16):
            xx, zz, cc = k // 4, (k // 2) % 2, k % 2
            t = qb[j, xx, zz, cc].astype(F32)
            at = 25 * k
            qf[at:at + 16, :] = t[:, 0:HW]
            qf[at + 16:at + 24, 0:512] = t[0:8, HW:QL]
            qf[at + 16:at + 24, 512:HW] = t[8:16, HW:HW + 384]
            for b in range(7):
                qf[at + 24:at + 25, 128 * b:128 * b + 128] = t[8 + b:9 + b, HW + 384:QL]
            u = ob[j, xx, zz, cc].astype(F32)
            of[14 * k:14 * k + 14, :] = u[0:14]
        qw[pl.ds(pl.multiple_of(400 * j, 16), 400), :] = qf[...].astype(BF16)
        ow[pl.ds(pl.multiple_of(224 * j, 16), 224), :] = of[...].astype(BF16)
        return carry

    lax.fori_loop(0, 4, unpack, 0)
    queries[...] = dot(normed[...], qw[...]).astype(BF16)
    ga[...] = dot_nt(go[...], ow[...]).astype(BF16)
    round_(6)
    round_(7)
    for s in range(2):
        for w in range(2, 4):
            step(w, s, 5)

    for clip in range(2):
        for n in range(1, FRAMES):
            frm = (f + n) % FRAMES
            place = pl.multiple_of(16 * frm, 16)
            got = lat.at[clip, pl.ds(place, 16), :]
            copy(got, got, pool_send.at[clip, frm], pool_recv.at[clip, frm], (dp, frm)).wait_recv()

    key_w = kb[...].reshape(V, HW)
    value_w = vb[...].reshape(V, HW)
    flat = lat[...].reshape(256, V)
    kl[...] = dot(flat, key_w).astype(BF16)
    vl[...] = dot(flat, value_w).astype(BF16)

    low = lax.broadcasted_iota(jnp.int32, (128, 128), 1) < HD
    scale = HD ** -0.5
    zero = jnp.zeros((128, 128), BF16)

    def split(block):
        return jnp.concatenate([jnp.where(low, block, zero), jnp.where(low, zero, block)], axis=0)

    def back_copy(clip, to, frm):
        rows = pl.multiple_of(16 * to, 16)
        return copy(
            back.at[clip, pl.ds(rows, 16), :], grad_pooled.at[2 * frm + clip],
            back_send.at[clip, to], back_recv.at[clip, frm], (dp, to))

    for clip in range(2):
        rows = slice(TP * clip, TP * clip + TP)
        lats = slice(128 * clip, 128 * clip + 128)
        for p in range(7):
            cols = slice(128 * p, 128 * p + 128)
            qp = queries[rows, cols]
            gp = ga[rows, cols]
            kd = split(kl[lats, cols])
            vd = split(vl[lats, cols])
            scores = dot_nt(kd, qp).reshape(2, 128, TP) * scale
            grad_probs = dot_nt(vd, gp).reshape(2, 128, TP)
            top = jnp.max(scores, axis=1, keepdims=True)
            shifted = jnp.exp(scores - top)
            probs = shifted / jnp.sum(shifted, axis=1, keepdims=True)
            probs_low = probs.astype(BF16)
            row_term = jnp.sum(probs_low.astype(F32) * grad_probs, axis=1, keepdims=True)
            grad_scores = (probs * (grad_probs - row_term) * scale).astype(BF16).reshape(256, TP)
            dk = dot(grad_scores, qp)
            dv = dot(probs_low.reshape(256, TP), gp)
            gk[lats, cols] = jnp.where(low, dk[0:128], dk[128:256]).astype(BF16)
            gv[lats, cols] = jnp.where(low, dv[0:128], dv[128:256]).astype(BF16)
            gq[rows, cols] = dot_tn(grad_scores, kd).astype(BF16)
        result = dot_nt(gk[lats, :], key_w) + dot_nt(gv[lats, :], value_w)
        back[clip] = result.astype(BF16)
        for n in range(1, FRAMES):
            back_copy(clip, (f + n) % FRAMES, f).start()
        mine = pl.multiple_of(16 * f, 16)
        pltpu.make_async_copy(
            back.at[clip, pl.ds(mine, 16), :], grad_pooled.at[2 * f + clip], own_sem.at[clip]
        ).start()

    grad_normed = dot_nt(gq[...], qw[...])
    for clip in range(2):
        rows = slice(TP * clip, TP * clip + TP)
        g = grad_normed[rows] * gain[0:1, :]
        unit_rows = unit[rows, :]
        mean_g = jnp.sum(g, axis=1, keepdims=True) * (1.0 / D)
        mean_gu = jnp.sum(g * unit_rows, axis=1, keepdims=True) * (1.0 / D)
        out = inverses[clip] * (g - mean_g - unit_rows * mean_gu)
        grad_text[clip] = out[0:TEXT, 0:D].astype(BF16)

    for moving in sends:
        moving.wait_send()
    for clip in range(2):
        for n in range(1, FRAMES):
            to = (f + n) % FRAMES
            pool_copy(clip, to, f).wait_send()
            back_copy(clip, to, f).wait_send()
        for n in range(1, FRAMES):
            frm = (f + n) % FRAMES
            got = grad_pooled.at[2 * frm + clip]
            copy(got, got, back_send.at[clip, frm], back_recv.at[clip, frm], (dp, frm)).wait_recv()
        mine = pl.multiple_of(16 * f, 16)
        pltpu.make_async_copy(
            back.at[clip, pl.ds(mine, 16), :], grad_pooled.at[2 * f + clip], own_sem.at[clip]
        ).wait()

    @pl.when(at_low)
    def _():
        for w in range(4):
            for k in range(4):
                cross(0, k, w, 4 + k).wait_send()

    @pl.when(at_high)
    def _():
        for w in range(4):
            for k in range(4):
                cross(1, k, w, 3 - k).wait_send()


def shards(video, pool_w, text, gain, lengths, cot, q_w, k_w, v_w, o_w):
    vmem = pl.BlockSpec(memory_space=pltpu.VMEM)
    smem = pl.BlockSpec(memory_space=pltpu.SMEM)
    dma = pltpu.SemaphoreType.DMA
    return pl.pallas_call(
        kernel,
        out_shape=(
            jax.ShapeDtypeStruct((2, TEXT, D), BF16),
            jax.ShapeDtypeStruct((16, LAT, V), BF16),
        ),
        in_specs=[vmem, vmem, vmem, vmem, smem, vmem, vmem, vmem, vmem, vmem],
        out_specs=(vmem, pl.BlockSpec(memory_space=pl.ANY)),
        scratch_shapes=[
            pltpu.VMEM((4, 4, 2, 2, 16, QL), BF16),
            pltpu.VMEM((4, 4, 2, 2, 16, DP), BF16),
            pltpu.VMEM((4, 4, 2, 2, 16, HW), BF16),
            pltpu.VMEM((4, 4, 2, 2, 16, HW), BF16),
            pltpu.VMEM((DP, HW), BF16),
            pltpu.VMEM((HW, DP), BF16),
            pltpu.VMEM((400, HW), F32),
            pltpu.VMEM((224, DP), F32),
            pltpu.VMEM((16, QL), F32),
            pltpu.VMEM((16, DP), F32),
            pltpu.VMEM((ROWS, DP), F32),
            pltpu.VMEM((ROWS, DP), F32),
            pltpu.VMEM((8, DP), F32),
            pltpu.VMEM((ROWS, DP), F32),
            pltpu.VMEM((ROWS, DP), BF16),
            pltpu.VMEM((ROWS, DP), BF16),
            pltpu.VMEM((ROWS, HW), BF16),
            pltpu.VMEM((ROWS, HW), BF16),
            pltpu.VMEM((256, V), BF16),
            pltpu.VMEM((2, 128, V), BF16),
            pltpu.VMEM((256, HW), BF16),
            pltpu.VMEM((256, HW), BF16),
            pltpu.VMEM((256, HW), BF16),
            pltpu.VMEM((256, HW), BF16),
            pltpu.VMEM((ROWS, HW), BF16),
            pltpu.VMEM((2, 128, V), BF16),
            dma((4, 2, 13)),
            dma((4, 2, 13)),
            dma((4, 4)),
            dma((4,)),
            dma((2, FRAMES)),
            dma((2, FRAMES)),
            dma((2, FRAMES)),
            dma((2, FRAMES)),
            dma((2,)),
        ],
        compiler_params=pltpu.CompilerParams(
            collective_id=0, has_side_effects=True, vmem_limit_bytes=52 * 1024 * 1024
        ),
    )(
        video.reshape(512, V), pool_w.reshape(LAT, 32), text, gain.reshape(1, D), lengths, cot,
        q_w, k_w, v_w, o_w,
    )


def solution(mesh):
    both = ("dp", "frame")
    return jax.shard_map(
        shards,
        mesh=mesh,
        in_specs=(
            P("dp", "frame", None, None), P("frame", None, None), P(both, None, None), P(), P(both),
            P(both, None, None), P("dp", None), P("dp", None), P("dp", None), P("dp", None),
        ),
        out_specs=(P(both, None, None), P("dp", "frame", None)),
        check_vma=False,
    )
```

```python
import functools

import jax
import jax.numpy as jnp
from jax import lax
from jax.experimental import pallas as pl
from jax.experimental.pallas import tpu as pltpu
from jax.sharding import PartitionSpec as P

HD = 64
EPSILON = 1e-05
MESH = pl.DeviceIdType.MESH
F32 = jnp.float32
BF16 = jnp.bfloat16

D = 1600
DP = 1664
V = 1024
HW = 896
TEXT = 77
TP = 80
QL = 1408
OL = 1536
LAT = 16
FRAMES = 8
ROWS = 2 * TP


def dot(left, right):
    return jnp.dot(left, right, preferred_element_type=F32)


def dot_nt(left, right):
    return lax.dot_general(left, right, (((1,), (1,)), ((), ())), preferred_element_type=F32)


def dot_tn(left, right):
    return lax.dot_general(left, right, (((0,), (0,)), ((), ())), preferred_element_type=F32)


def kernel(
    video, pool_w, text, gain_in, lengths, cot, q_in, k_in, v_in, o_in,
    grad_text, grad_pooled,
    qb, ob, kb, vb, qw, ow, qf, of, qs, os_, xs, cs, gain, unit, normed, go, queries, ga,
    pooled, lat, kl, vl, gk, gv, gq, back,
    send, recv, cross_send, cross_recv, pool_send, pool_recv, back_send, back_recv, own_sem, in_sem, text_in, cot_in, video_in, q_own, o_own, probs_all,
):
    dp = lax.axis_index("dp")
    f = lax.axis_index("frame")
    y, x, h, c = dp // 16, (dp // 4) % 4, (dp // 2) % 2, dp % 2
    o = 1 - h

    def device(y, x, h, c, f):
        return (((y * 4 + x) * 2 + h) * 2 + c, f)

    def up(i):
        return (i + 1) % 4

    def down(i):
        return (i + 3) % 4

    def far(i):
        return (i + 2) % 4

    sibling = device(y, x, h, 1 - c, f)
    x_up, x_down = device(y, up(x), h, c, f), device(y, down(x), h, c, f)
    y_up, y_down = device(up(y), x, h, c, f), device(down(y), x, h, c, f)

    x_far, y_far = device(y, far(x), h, c, f), device(far(y), x, h, c, f)

    def spread_rows(ref, t, pair):
        for j in range(12):
            ref[j, 2 * t:2 * t + 2, :] = pair[:, 128 * j:128 * j + 128]
        ref[12, 2 * t:2 * t + 2, 0:64] = pair[:, 1536:D]

    def clip_rows(ref, clip):
        return jnp.concatenate([ref[j, pl.ds(clip, TP, stride=2), :] for j in range(13)], axis=1)

    barrier = pltpu.get_barrier_semaphore()

    def greet(who):
        pl.semaphore_signal(barrier, inc=1, device_id=who, device_id_type=MESH)

    for who in (sibling, x_up, x_down, x_far, y_up, y_down, y_far):
        greet(who)
    for step in range(1, FRAMES):
        greet((dp, (f + step) % FRAMES))
    other_dp = device(y, x, o, c, f)[0]
    at_low = f == 0
    at_high = f == FRAMES - 1
    at_end = jnp.logical_or(at_low, at_high)

    @pl.when(at_low)
    def _():
        for k in range(4):
            greet((other_dp, 7 - k))

    @pl.when(at_high)
    def _():
        for k in range(4):
            greet((other_dp, k))

    @pl.when(jnp.logical_not(at_end))
    def _():
        greet((other_dp, jnp.where(f < 4, FRAMES - 1, 0)))

    k_copy = pltpu.make_async_copy(k_in, kb.at[y, x, h, c], in_sem.at[5])
    v_copy = pltpu.make_async_copy(v_in, vb.at[y, x, h, c], in_sem.at[6])
    q_copy = pltpu.make_async_copy(q_in, q_own, in_sem.at[3])
    o_copy = pltpu.make_async_copy(o_in, o_own, in_sem.at[4])
    for coming in (o_copy, q_copy, k_copy, v_copy):
        coming.start()
    video_copy = pltpu.make_async_copy(video, video_in, in_sem.at[0])
    video_copy.start()
    text_copy = pltpu.make_async_copy(text, text_in, in_sem.at[1])
    text_copy.start()
    cot_copy = pltpu.make_async_copy(cot, cot_in, in_sem.at[2])
    cot_copy.start()

    qs[...] = jnp.zeros_like(qs)
    os_[...] = jnp.zeros_like(os_)
    o_copy.wait()
    q_copy.wait()
    q = q_own[...].astype(F32)
    qs[:, 0:HW] = q[0:16]
    qs[0:8, HW:QL] = q[16:24, 0:512]
    qs[8:16, HW:HW + 384] = q[16:24, 512:HW]
    for b in range(7):
        qs[8 + b:9 + b, HW + 384:QL] = q[24:25, 128 * b:128 * b + 128]
    qb[y, x, h, c] = qs[...].astype(BF16)
    rest = o_own[...].astype(F32)
    os_[0:14, :] = rest[:, 0:OL]
    for b in range(7):
        os_[14:16, 128 * b:128 * b + 64] = rest[2 * b:2 * b + 2, OL:D]
    ob[y, x, h, c] = os_[...].astype(BF16)
    k_copy.wait()
    v_copy.wait()

    count = 14 + jnp.where(at_end, 4, 1)
    pl.semaphore_wait(barrier, count)

    bufs = (qb, ob, kb, vb)
    x_first = (True, False, False, True)
    sends = []

    def copy(src, dst, s_sem, r_sem, who):
        return pltpu.make_async_remote_copy(
            src_ref=src, dst_ref=dst, send_sem=s_sem, recv_sem=r_sem, device_id=who,
            device_id_type=MESH)

    def parts(w):
        buf = bufs[w]
        if x_first[w]:
            return (
                lambda a, z: buf.at[y, a, z, c],
                lambda b, z: buf.at[b, :, z, c],
                lambda b, z, k: buf.at[b, pl.ds(2 * k, 2), z, c],
                (lambda b, z: buf.at[b, :, z, 1 - c]),
                x, y, x_up, x_down, x_far, y_up, y_down,
            )
        return (
            lambda a, z: buf.at[a, x, z, c],
            lambda b, z: buf.at[:, b, z, c],
            lambda b, z, k: buf.at[pl.ds(2 * k, 2), b, z, c],
            (lambda b, z: buf.at[:, b, z, 1 - c]),
            y, x, y_up, y_down, y_far, x_up, x_down,
        )

    def step(w, s, k):
        item, row, pair, other_row, a, b, a_up, a_down, a_far, b_up, b_down = parts(w)
        z = h if s == 0 else o

        def go_(ref, index, who):
            moving = copy(ref, ref, send.at[w, s, index], recv.at[w, s, index], who)
            moving.start()
            sends.append(moving)

        def come(ref, index, who):
            copy(ref, ref, send.at[w, s, index], recv.at[w, s, index], who).wait_recv()

        if k == 0:
            if s == 1:
                mine = bufs[w].at[y, x, o, c]
                copy(mine, mine, cross_send.at[w, 0], cross_recv.at[w], (other_dp, f)).wait_recv()
            go_(item(a, z), 0, a_up)
            go_(item(a, z), 1, a_down)
            go_(item(a, z), 2, a_far)
        elif k == 1:
            come(item(down(a), z), 0, a_up)
            come(item(up(a), z), 1, a_down)
            come(item(far(a), z), 2, a_far)
            go_(pair(b, z, 0), 3, b_up)
            go_(pair(b, z, 1), 6, b_down)
            go_(row(b, z), 9, sibling)
        elif k == 2:
            come(pair(down(b), z, 0), 3, b_up)
            go_(pair(down(b), z, 0), 7, b_up)
            come(pair(up(b), z, 1), 6, b_down)
            go_(pair(up(b), z, 1), 8, b_down)
            go_(pair(b, z, 1), 4, b_up)
            go_(pair(b, z, 0), 5, b_down)
        elif k == 3:
            come(pair(down(b), z, 1), 4, b_up)
            go_(row(down(b), z), 10, sibling)
            come(pair(up(b), z, 0), 5, b_down)
            go_(row(up(b), z), 11, sibling)
            come(pair(far(b), z, 0), 7, b_up)
            come(pair(far(b), z, 1), 8, b_down)
            go_(row(far(b), z), 12, sibling)
        else:
            for n, at in enumerate((b, down(b), up(b), far(b))):
                ref = other_row(at, z)
                copy(ref, ref, send.at[w, s, 9 + n], recv.at[w, s, 9 + n], sibling).wait_recv()

    def steps(k, s, *which):
        for w in which:
            step(w, s, k)

    steps(0, 0, 0, 2)

    def cross(where, k, w, target):
        mine = bufs[w].at[y, x, h, c]
        return copy(mine, mine, cross_send.at[w, k], cross_recv.at[w], (other_dp, target))

    def start_cross(which):
        @pl.when(at_low)
        def _():
            for w in which:
                for k in range(4):
                    cross(0, k, w, 4 + k).start()

        @pl.when(at_high)
        def _():
            for w in which:
                for k in range(4):
                    cross(1, k, w, 3 - k).start()

    start_cross((0, 2))
    steps(0, 0, 3, 1)

    i0 = lax.broadcasted_iota(jnp.int32, (32, 256), 0)
    i1 = lax.broadcasted_iota(jnp.int32, (32, 256), 1)
    spread = jnp.where(i1 % 32 == i0, 1.0, 0.0).astype(BF16)
    wide = dot(pool_w[...], spread)
    wide = jnp.concatenate([wide] * 8, axis=0)
    j0 = lax.broadcasted_iota(jnp.int32, (128, 256), 0)
    j1 = lax.broadcasted_iota(jnp.int32, (128, 256), 1)
    diag = jnp.where(j0 // 16 == j1 // 32, wide, 0.0).astype(BF16)
    video_copy.wait()
    for half in range(2):
        part = dot(diag, video_in[256 * half:256 * half + 256, :])
        pooled[128 * half:128 * half + 128, :] = part.astype(BF16)

    def pool_copy(clip, to, frm):
        start = pl.multiple_of(32 * to + 16 * clip, 16)
        place = pl.multiple_of(16 * frm, 16)
        return copy(
            pooled.at[pl.ds(start, 16), :], lat.at[clip, pl.ds(place, 16), :],
            pool_send.at[clip, to], pool_recv.at[clip, frm], (dp, to))

    for clip in range(2):
        for n in range(1, FRAMES):
            pool_copy(clip, (f + n) % FRAMES, f).start()
        start = pl.multiple_of(32 * f + 16 * clip, 16)
        place = pl.multiple_of(16 * f, 16)
        lat[clip, pl.ds(place, 16), :] = pooled[pl.ds(start, 16), :]

    steps(1, 0, 2, 0, 3, 1)
    start_cross((3, 1))
    gain[...] = jnp.zeros_like(gain)
    gain[0:1, 0:D] = gain_in[...].reshape(1, D)
    xs[...] = jnp.zeros_like(xs)
    text_copy.wait()
    for t in range(TEXT):
        spread_rows(xs, t, text_in[t].astype(F32))
    steps(2, 0, 2, 0)
    cs[...] = jnp.zeros_like(cs)
    cot_copy.wait()
    for t in range(TEXT):
        spread_rows(cs, t, cot_in[t].astype(F32))
    steps(2, 0, 3, 1)
    steps(0, 1, 2, 0)
    lane = lax.broadcasted_iota(jnp.int32, (TP, DP), 1)
    position = lax.broadcasted_iota(jnp.int32, (TP, DP), 0)
    inverses = []
    for clip in range(2):
        rows = slice(TP * clip, TP * clip + TP)
        states = clip_rows(xs, clip)
        average = jnp.sum(states, axis=1, keepdims=True) * (1.0 / D)
        centered = jnp.where(lane < D, states - average, 0.0)
        square = jnp.sum(centered * centered, axis=1, keepdims=True) * (1.0 / D)
        inverse = lax.rsqrt(square + EPSILON)
        inverses.append(inverse)
        unit_rows = centered * inverse
        unit[rows, :] = unit_rows
        normed[rows, :] = (unit_rows * gain[0:1, :]).astype(BF16)
        go[rows, :] = jnp.where(position < lengths[clip], clip_rows(cs, clip), 0.0).astype(BF16)
        if clip == 0:
            steps(0, 1, 3, 1)
    steps(1, 1, 2, 0)
    steps(3, 0, 2, 0, 3, 1)
    steps(1, 1, 3, 1)
    steps(2, 1, 2, 0)

    qw[D:DP, :] = jnp.zeros((DP - D, HW), BF16)

    of[...] = jnp.zeros_like(of)

    def unpack_q(zz):
        def body(j, carry):
            for xx in range(4):
                for cc in range(2):
                    at = 25 * (4 * xx + 2 * zz + cc)
                    t = qb[j, xx, zz, cc].astype(F32)
                    qf[j, at:at + 16, :] = t[:, 0:HW]
                    qf[j, at + 16:at + 24, 0:512] = t[0:8, HW:QL]
                    qf[j, at + 16:at + 24, 512:HW] = t[8:16, HW:HW + 384]
                    for b in range(7):
                        qf[j, at + 24:at + 25, 128 * b:128 * b + 128] = t[8 + b:9 + b, HW + 384:QL]
            return carry

        lax.fori_loop(0, 4, body, 0)

    def unpack_o(zz):
        def body(j, carry):
            for xx in range(4):
                for cc in range(2):
                    at = 14 * (4 * xx + 2 * zz + cc)
                    t = ob[j, xx, zz, cc].astype(F32)
                    of[j, at:at + 14, 0:OL] = t[0:14]
                    for b in range(7):
                        of[j, at + 2 * b:at + 2 * b + 2, OL:D] = t[14:16, 128 * b:128 * b + 64]
            return carry

        lax.fori_loop(0, 4, body, 0)

    def unpack_part(unpack, mine):
        for zz in range(2):
            @pl.when((h == zz) if mine else (h != zz))
            def _(zz=zz):
                unpack(zz)

    steps(4, 0, 0)
    unpack_part(unpack_q, True)
    steps(2, 1, 3, 1)
    steps(4, 0, 1)
    unpack_part(unpack_o, True)
    steps(3, 1, 2, 0)
    steps(4, 0, 2)
    steps(4, 1, 2, 0)
    unpack_part(unpack_q, False)
    for j in range(4):
        qw[400 * j:400 * j + 400, :] = qf[j].astype(BF16)
    queries[...] = dot(normed[...], qw[...]).astype(BF16)

    for clip in range(2):
        for n in range(1, FRAMES):
            frm = (f + n) % FRAMES
            place = pl.multiple_of(16 * frm, 16)
            got = lat.at[clip, pl.ds(place, 16), :]
            copy(got, got, pool_send.at[clip, frm], pool_recv.at[clip, frm], (dp, frm)).wait_recv()

    kl[...] = dot(lat[...].reshape(256, V), kb[...].reshape(V, HW)).astype(BF16)

    low = lax.broadcasted_iota(jnp.int32, (128, 128), 1) < HD
    scale = HD ** -0.5
    zero = jnp.zeros((128, 128), BF16)

    def split(block):
        return jnp.concatenate([jnp.where(low, block, zero), jnp.where(low, zero, block)], axis=0)

    for clip in range(2):
        rows = slice(TP * clip, TP * clip + TP)
        lats = slice(128 * clip, 128 * clip + 128)
        for p in range(7):
            cols = slice(128 * p, 128 * p + 128)
            scores = dot_nt(split(kl[lats, cols]), queries[rows, cols]).reshape(2, 128, TP) * scale
            top = jnp.max(scores, axis=1, keepdims=True)
            shifted = jnp.exp(scores - top)
            probs_all[7 * clip + p] = shifted / jnp.sum(shifted, axis=1, keepdims=True)

    steps(3, 1, 3, 1)
    steps(4, 0, 3)
    steps(4, 1, 1)
    unpack_part(unpack_o, False)
    for j in range(4):
        ow[224 * j:224 * j + 224, :] = of[j].astype(BF16)
    ga[...] = dot_nt(go[...], ow[...]).astype(BF16)
    steps(4, 1, 3)
    key_w = kb[...].reshape(V, HW)
    value_w = vb[...].reshape(V, HW)
    vl[...] = dot(lat[...].reshape(256, V), value_w).astype(BF16)

    def back_copy(clip, to, frm):
        rows = pl.multiple_of(16 * to, 16)
        return copy(
            back.at[clip, pl.ds(rows, 16), :], grad_pooled.at[2 * frm + clip],
            back_send.at[clip, to], back_recv.at[clip, frm], (dp, to))

    for clip in range(2):
        rows = slice(TP * clip, TP * clip + TP)
        lats = slice(128 * clip, 128 * clip + 128)
        for p in range(7):
            cols = slice(128 * p, 128 * p + 128)
            qp = queries[rows, cols]
            gp = ga[rows, cols]
            kd = split(kl[lats, cols])
            vd = split(vl[lats, cols])
            grad_probs = dot_nt(vd, gp).reshape(2, 128, TP)
            probs = probs_all[7 * clip + p]
            probs_low = probs.astype(BF16)
            row_term = jnp.sum(probs_low.astype(F32) * grad_probs, axis=1, keepdims=True)
            grad_scores = (probs * (grad_probs - row_term) * scale).astype(BF16).reshape(256, TP)
            dk = dot(grad_scores, qp)
            dv = dot(probs_low.reshape(256, TP), gp)
            gk[lats, cols] = jnp.where(low, dk[0:128], dk[128:256]).astype(BF16)
            gv[lats, cols] = jnp.where(low, dv[0:128], dv[128:256]).astype(BF16)
            gq[rows, cols] = dot_tn(grad_scores, kd).astype(BF16)
        result = dot_nt(gk[lats, :], key_w) + dot_nt(gv[lats, :], value_w)
        back[clip] = result.astype(BF16)
        for n in range(1, FRAMES):
            back_copy(clip, (f + n) % FRAMES, f).start()
        mine = pl.multiple_of(16 * f, 16)
        pltpu.make_async_copy(
            back.at[clip, pl.ds(mine, 16), :], grad_pooled.at[2 * f + clip], own_sem.at[clip]
        ).start()

    grad_normed = dot_nt(gq[...], qw[...])
    for clip in range(2):
        rows = slice(TP * clip, TP * clip + TP)
        g = grad_normed[rows] * gain[0:1, :]
        unit_rows = unit[rows, :]
        mean_g = jnp.sum(g, axis=1, keepdims=True) * (1.0 / D)
        mean_gu = jnp.sum(g * unit_rows, axis=1, keepdims=True) * (1.0 / D)
        out = inverses[clip] * (g - mean_g - unit_rows * mean_gu)
        for j in range(13):
            xs[j, pl.ds(clip, TP, stride=2), :] = out[:, 128 * j:128 * j + 128]
    for t in range(TEXT):
        both = jnp.concatenate([xs[j, 2 * t:2 * t + 2, :] for j in range(13)], axis=1)
        grad_text[t] = both[:, 0:D].astype(BF16)

    for moving in sends:
        moving.wait_send()
    for clip in range(2):
        for n in range(1, FRAMES):
            to = (f + n) % FRAMES
            pool_copy(clip, to, f).wait_send()
            back_copy(clip, to, f).wait_send()
        for n in range(1, FRAMES):
            frm = (f + n) % FRAMES
            got = grad_pooled.at[2 * frm + clip]
            copy(got, got, back_send.at[clip, frm], back_recv.at[clip, frm], (dp, frm)).wait_recv()
        mine = pl.multiple_of(16 * f, 16)
        pltpu.make_async_copy(
            back.at[clip, pl.ds(mine, 16), :], grad_pooled.at[2 * f + clip], own_sem.at[clip]
        ).wait()

    @pl.when(at_low)
    def _():
        for w in range(4):
            for k in range(4):
                cross(0, k, w, 4 + k).wait_send()

    @pl.when(at_high)
    def _():
        for w in range(4):
            for k in range(4):
                cross(1, k, w, 3 - k).wait_send()


def shards(video, pool_w, text, gain, lengths, cot, q_w, k_w, v_w, o_w):
    vmem = pl.BlockSpec(memory_space=pltpu.VMEM)
    smem = pl.BlockSpec(memory_space=pltpu.SMEM)
    dma = pltpu.SemaphoreType.DMA
    anywhere = pl.BlockSpec(memory_space=pl.ANY)
    grad_text, grad_pooled = pl.pallas_call(
        kernel,
        out_shape=(
            jax.ShapeDtypeStruct((TEXT, 2, D), BF16),
            jax.ShapeDtypeStruct((16, LAT, V), BF16),
        ),
        in_specs=[anywhere, vmem, anywhere, vmem, smem, anywhere, anywhere, anywhere, anywhere, anywhere],
        out_specs=(vmem, anywhere),
        scratch_shapes=[
            pltpu.VMEM((4, 4, 2, 2, 16, QL), BF16),
            pltpu.VMEM((4, 4, 2, 2, 16, OL), BF16),
            pltpu.VMEM((4, 4, 2, 2, 16, HW), BF16),
            pltpu.VMEM((4, 4, 2, 2, 16, HW), BF16),
            pltpu.VMEM((DP, HW), BF16),
            pltpu.VMEM((HW, DP), BF16),
            pltpu.VMEM((4, 400, HW), F32),
            pltpu.VMEM((4, 224, DP), F32),
            pltpu.VMEM((16, QL), F32),
            pltpu.VMEM((16, OL), F32),
            pltpu.VMEM((13, ROWS, 128), F32),
            pltpu.VMEM((13, ROWS, 128), F32),
            pltpu.VMEM((8, DP), F32),
            pltpu.VMEM((ROWS, DP), F32),
            pltpu.VMEM((ROWS, DP), BF16),
            pltpu.VMEM((ROWS, DP), BF16),
            pltpu.VMEM((ROWS, HW), BF16),
            pltpu.VMEM((ROWS, HW), BF16),
            pltpu.VMEM((256, V), BF16),
            pltpu.VMEM((2, 128, V), BF16),
            pltpu.VMEM((256, HW), BF16),
            pltpu.VMEM((256, HW), BF16),
            pltpu.VMEM((256, HW), BF16),
            pltpu.VMEM((256, HW), BF16),
            pltpu.VMEM((ROWS, HW), BF16),
            pltpu.VMEM((2, 128, V), BF16),
            dma((4, 2, 13)),
            dma((4, 2, 13)),
            dma((4, 4)),
            dma((4,)),
            dma((2, FRAMES)),
            dma((2, FRAMES)),
            dma((2, FRAMES)),
            dma((2, FRAMES)),
            dma((2,)),
            dma((7,)),
            pltpu.VMEM((TEXT, 2, D), BF16),
            pltpu.VMEM((TEXT, 2, D), BF16),
            pltpu.VMEM((512, V), BF16),
            pltpu.VMEM((25, HW), BF16),
            pltpu.VMEM((14, D), BF16),
            pltpu.VMEM((14, 2, 128, TP), F32),
        ],
        compiler_params=pltpu.CompilerParams(
            collective_id=0, has_side_effects=True, vmem_limit_bytes=60 * 1024 * 1024
        ),
    )(
        video.reshape(512, V), pool_w.reshape(LAT, 32), text.transpose(1, 0, 2), gain, lengths,
        cot.transpose(1, 0, 2), q_w, k_w, v_w, o_w,
    )
    return grad_text.transpose(1, 0, 2), grad_pooled


def solution(mesh):
    both = ("dp", "frame")
    return jax.shard_map(
        shards,
        mesh=mesh,
        in_specs=(
            P("dp", "frame", None, None), P("frame", None, None), P(both, None, None), P(), P(both),
            P(both, None, None), P("dp", None), P("dp", None), P("dp", None), P("dp", None),
        ),
        out_specs=(P(both, None, None), P("dp", "frame", None)),
        check_vma=False,
    )
```

```python
import functools

import jax
import jax.numpy as jnp
from jax import lax
from jax.experimental import pallas as pl
from jax.experimental.pallas import tpu as pltpu
from jax.sharding import PartitionSpec as P

HD = 64
EPSILON = 1e-05
MESH = pl.DeviceIdType.MESH
F32 = jnp.float32
BF16 = jnp.bfloat16

D = 1600
DP = 1664
V = 1024
HW = 896
TEXT = 77
TP = 80
QL = 1408
OL = 1536
LAT = 16
FRAMES = 8
ROWS = 2 * TP


def dot(left, right):
    return jnp.dot(left, right, preferred_element_type=F32)


def dot_nt(left, right):
    return lax.dot_general(left, right, (((1,), (1,)), ((), ())), preferred_element_type=F32)


def dot_tn(left, right):
    return lax.dot_general(left, right, (((0,), (0,)), ((), ())), preferred_element_type=F32)


def kernel(
    video, pool_w, text, gain_in, lengths, cot, q_in, k_in, v_in, o_in,
    grad_text, grad_pooled,
    qb, ob, kb, vb, qw, ow, qf, of, qs, os_, xs, cs, gain, unit, normed, go, queries, ga,
    pooled, lat, kl, vl, gk, gv, gq, back,
    send, recv, cross_send, cross_recv, pool_send, pool_recv, back_send, back_recv, own_sem, in_sem, text_in, cot_in, video_in, q_own, o_own, probs_all,
):
    dp = lax.axis_index("dp")
    f = lax.axis_index("frame")
    y, x, h, c = dp // 16, (dp // 4) % 4, (dp // 2) % 2, dp % 2
    o = 1 - h

    def device(y, x, h, c, f):
        return (((y * 4 + x) * 2 + h) * 2 + c, f)

    def up(i):
        return (i + 1) % 4

    def down(i):
        return (i + 3) % 4

    def far(i):
        return (i + 2) % 4

    sibling = device(y, x, h, 1 - c, f)
    x_up, x_down = device(y, up(x), h, c, f), device(y, down(x), h, c, f)
    y_up, y_down = device(up(y), x, h, c, f), device(down(y), x, h, c, f)

    x_far, y_far = device(y, far(x), h, c, f), device(far(y), x, h, c, f)

    def spread_rows(ref, t, pair):
        for j in range(12):
            ref[j, 2 * t:2 * t + 2, :] = pair[:, 128 * j:128 * j + 128]
        ref[12, 2 * t:2 * t + 2, 0:64] = pair[:, 1536:D]

    def clip_rows(ref, clip):
        return jnp.concatenate([ref[j, pl.ds(clip, TP, stride=2), :] for j in range(13)], axis=1)

    barrier = pltpu.get_barrier_semaphore()

    def greet(who):
        pl.semaphore_signal(barrier, inc=1, device_id=who, device_id_type=MESH)

    for who in (sibling, x_up, x_down, x_far, y_up, y_down, y_far):
        greet(who)
    for step in range(1, FRAMES):
        greet((dp, (f + step) % FRAMES))
    other_dp = device(y, x, o, c, f)[0]
    at_low = f == 0
    at_high = f == FRAMES - 1
    at_end = jnp.logical_or(at_low, at_high)

    @pl.when(at_low)
    def _():
        for k in range(4):
            greet((other_dp, 7 - k))

    @pl.when(at_high)
    def _():
        for k in range(4):
            greet((other_dp, k))

    @pl.when(jnp.logical_not(at_end))
    def _():
        greet((other_dp, jnp.where(f < 4, FRAMES - 1, 0)))

    k_copy = pltpu.make_async_copy(k_in, kb.at[y, x, h, c], in_sem.at[5])
    v_copy = pltpu.make_async_copy(v_in, vb.at[y, x, h, c], in_sem.at[6])
    q_copy = pltpu.make_async_copy(q_in, q_own, in_sem.at[3])
    o_copy = pltpu.make_async_copy(o_in, o_own, in_sem.at[4])
    for coming in (o_copy, q_copy, k_copy, v_copy):
        coming.start()
    video_copy = pltpu.make_async_copy(video, video_in, in_sem.at[0])
    video_copy.start()
    text_copy = pltpu.make_async_copy(text, text_in, in_sem.at[1])
    text_copy.start()
    cot_copy = pltpu.make_async_copy(cot, cot_in, in_sem.at[2])
    cot_copy.start()

    qs[...] = jnp.zeros_like(qs)
    os_[...] = jnp.zeros_like(os_)
    o_copy.wait()
    q_copy.wait()
    q = q_own[...].astype(F32)
    qs[:, 0:HW] = q[0:16]
    qs[0:8, HW:QL] = q[16:24, 0:512]
    qs[8:16, HW:HW + 384] = q[16:24, 512:HW]
    for b in range(7):
        qs[8 + b:9 + b, HW + 384:QL] = q[24:25, 128 * b:128 * b + 128]
    qb[y, x, h, c] = qs[...].astype(BF16)
    rest = o_own[...].astype(F32)
    os_[0:14, :] = rest[:, 0:OL]
    for b in range(7):
        os_[14:16, 128 * b:128 * b + 64] = rest[2 * b:2 * b + 2, OL:D]
    ob[y, x, h, c] = os_[...].astype(BF16)
    k_copy.wait()
    v_copy.wait()

    count = 14 + jnp.where(at_end, 4, 1)
    pl.semaphore_wait(barrier, count)

    bufs = (qb, ob, kb, vb)
    x_first = (True, False, False, True)
    sends = []

    def copy(src, dst, s_sem, r_sem, who):
        return pltpu.make_async_remote_copy(
            src_ref=src, dst_ref=dst, send_sem=s_sem, recv_sem=r_sem, device_id=who,
            device_id_type=MESH)

    def parts(w):
        buf = bufs[w]
        if x_first[w]:
            return (
                lambda a, z: buf.at[y, a, z, c],
                lambda b, z: buf.at[b, :, z, c],
                lambda b, z, k: buf.at[b, pl.ds(2 * k, 2), z, c],
                lambda b, z: buf.at[b, :, z, 1 - c],
                lambda b, z, k: buf.at[b, pl.ds(2 * k, 2), z, 1 - c],
                x, y, x_up, x_down, x_far, y_up, y_down,
            )
        return (
            lambda a, z: buf.at[a, x, z, c],
            lambda b, z: buf.at[:, b, z, c],
            lambda b, z, k: buf.at[pl.ds(2 * k, 2), b, z, c],
            lambda b, z: buf.at[:, b, z, 1 - c],
            lambda b, z, k: buf.at[pl.ds(2 * k, 2), b, z, 1 - c],
            y, x, y_up, y_down, y_far, x_up, x_down,
        )

    def step(w, s, k):
        item, row, pair, other_row, other_pair, a, b, a_up, a_down, a_far, b_up, b_down = parts(w)
        z = h if s == 0 else o

        def go_(ref, index, who):
            moving = copy(ref, ref, send.at[w, s, index], recv.at[w, s, index], who)
            moving.start()
            sends.append(moving)

        def come(ref, index, who):
            copy(ref, ref, send.at[w, s, index], recv.at[w, s, index], who).wait_recv()

        if k == 0:
            if s == 1:
                mine = bufs[w].at[y, x, o, c]
                copy(mine, mine, cross_send.at[w, 0], cross_recv.at[w], (other_dp, f)).wait_recv()
            go_(item(a, z), 0, a_up)
            go_(item(a, z), 1, a_down)
            go_(item(a, z), 2, a_far)
        elif k == 1:
            come(item(down(a), z), 0, a_up)
            come(item(up(a), z), 1, a_down)
            come(item(far(a), z), 2, a_far)
            go_(pair(b, z, 0), 3, b_up)
            go_(pair(b, z, 1), 6, b_down)
            go_(row(b, z), 9, sibling)
        elif k == 2:
            come(pair(down(b), z, 0), 3, b_up)
            go_(pair(down(b), z, 0), 7, b_up)
            come(pair(up(b), z, 1), 6, b_down)
            go_(pair(up(b), z, 1), 8, b_down)
            go_(pair(b, z, 1), 4, b_up)
            go_(pair(b, z, 0), 5, b_down)
            go_(pair(down(b), z, 0), 10, sibling)
            go_(pair(up(b), z, 1), 11, sibling)
        elif k == 3:
            come(pair(down(b), z, 1), 4, b_up)
            go_(pair(down(b), z, 1), 12, sibling)
            come(pair(up(b), z, 0), 5, b_down)
            go_(pair(up(b), z, 0), 13, sibling)
            come(pair(far(b), z, 0), 7, b_up)
            go_(pair(far(b), z, 0), 14, sibling)
            come(pair(far(b), z, 1), 8, b_down)
            go_(pair(far(b), z, 1), 15, sibling)
        else:
            refs = (other_row(b, z), other_pair(down(b), z, 0), other_pair(up(b), z, 1),
                    other_pair(down(b), z, 1), other_pair(up(b), z, 0),
                    other_pair(far(b), z, 0), other_pair(far(b), z, 1))
            for n, ref in enumerate(refs):
                copy(ref, ref, send.at[w, s, 9 + n], recv.at[w, s, 9 + n], sibling).wait_recv()

    def steps(k, s, *which):
        for w in which:
            step(w, s, k)

    steps(0, 0, 0, 2)

    def cross(where, k, w, target):
        mine = bufs[w].at[y, x, h, c]
        return copy(mine, mine, cross_send.at[w, k], cross_recv.at[w], (other_dp, target))

    def start_cross(which):
        @pl.when(at_low)
        def _():
            for w in which:
                for k in range(4):
                    cross(0, k, w, 4 + k).start()

        @pl.when(at_high)
        def _():
            for w in which:
                for k in range(4):
                    cross(1, k, w, 3 - k).start()

    start_cross((0, 2))
    steps(0, 0, 3, 1)

    i0 = lax.broadcasted_iota(jnp.int32, (32, 256), 0)
    i1 = lax.broadcasted_iota(jnp.int32, (32, 256), 1)
    spread = jnp.where(i1 % 32 == i0, 1.0, 0.0).astype(BF16)
    wide = dot(pool_w[...], spread)
    wide = jnp.concatenate([wide] * 8, axis=0)
    j0 = lax.broadcasted_iota(jnp.int32, (128, 256), 0)
    j1 = lax.broadcasted_iota(jnp.int32, (128, 256), 1)
    diag = jnp.where(j0 // 16 == j1 // 32, wide, 0.0).astype(BF16)
    video_copy.wait()
    for half in range(2):
        part = dot(diag, video_in[256 * half:256 * half + 256, :])
        pooled[128 * half:128 * half + 128, :] = part.astype(BF16)

    start_cross((3, 1))

    def pool_copy(clip, to, frm):
        start = pl.multiple_of(32 * to + 16 * clip, 16)
        place = pl.multiple_of(16 * frm, 16)
        return copy(
            pooled.at[pl.ds(start, 16), :], lat.at[clip, pl.ds(place, 16), :],
            pool_send.at[clip, to], pool_recv.at[clip, frm], (dp, to))

    for clip in range(2):
        for n in range(1, FRAMES):
            pool_copy(clip, (f + n) % FRAMES, f).start()
        start = pl.multiple_of(32 * f + 16 * clip, 16)
        place = pl.multiple_of(16 * f, 16)
        lat[clip, pl.ds(place, 16), :] = pooled[pl.ds(start, 16), :]

    steps(1, 0, 2, 0, 3, 1)
    gain[...] = jnp.zeros_like(gain)
    gain[0:1, 0:D] = gain_in[...].reshape(1, D)
    xs[...] = jnp.zeros_like(xs)
    text_copy.wait()
    for t in range(TEXT):
        spread_rows(xs, t, text_in[t].astype(F32))
    steps(2, 0, 2, 0)
    cs[...] = jnp.zeros_like(cs)
    cot_copy.wait()
    for t in range(TEXT):
        spread_rows(cs, t, cot_in[t].astype(F32))
    steps(2, 0, 3, 1)
    steps(0, 1, 2, 0)
    lane = lax.broadcasted_iota(jnp.int32, (TP, DP), 1)
    position = lax.broadcasted_iota(jnp.int32, (TP, DP), 0)
    inverses = []
    for clip in range(2):
        rows = slice(TP * clip, TP * clip + TP)
        states = clip_rows(xs, clip)
        average = jnp.sum(states, axis=1, keepdims=True) * (1.0 / D)
        centered = jnp.where(lane < D, states - average, 0.0)
        square = jnp.sum(centered * centered, axis=1, keepdims=True) * (1.0 / D)
        inverse = lax.rsqrt(square + EPSILON)
        inverses.append(inverse)
        unit_rows = centered * inverse
        unit[rows, :] = unit_rows
        normed[rows, :] = (unit_rows * gain[0:1, :]).astype(BF16)
        go[rows, :] = jnp.where(position < lengths[clip], clip_rows(cs, clip), 0.0).astype(BF16)
        if clip == 0:
            steps(0, 1, 3, 1)
    steps(1, 1, 2, 0)
    steps(3, 0, 2, 0, 3, 1)
    steps(1, 1, 3, 1)
    steps(2, 1, 2, 0)

    qw[D:DP, :] = jnp.zeros((DP - D, HW), BF16)

    of[...] = jnp.zeros_like(of)

    def unpack_q(zz):
        def body(j, carry):
            for xx in range(4):
                for cc in range(2):
                    at = 25 * (4 * xx + 2 * zz + cc)
                    t = qb[j, xx, zz, cc].astype(F32)
                    qf[j, at:at + 16, :] = t[:, 0:HW]
                    qf[j, at + 16:at + 24, 0:512] = t[0:8, HW:QL]
                    qf[j, at + 16:at + 24, 512:HW] = t[8:16, HW:HW + 384]
                    for b in range(7):
                        qf[j, at + 24:at + 25, 128 * b:128 * b + 128] = t[8 + b:9 + b, HW + 384:QL]
            return carry

        lax.fori_loop(0, 4, body, 0)

    def unpack_o(zz):
        def body(j, carry):
            for xx in range(4):
                for cc in range(2):
                    at = 14 * (4 * xx + 2 * zz + cc)
                    t = ob[j, xx, zz, cc].astype(F32)
                    of[j, at:at + 14, 0:OL] = t[0:14]
                    for b in range(7):
                        of[j, at + 2 * b:at + 2 * b + 2, OL:D] = t[14:16, 128 * b:128 * b + 64]
            return carry

        lax.fori_loop(0, 4, body, 0)

    def unpack_part(unpack, mine):
        for zz in range(2):
            @pl.when((h == zz) if mine else (h != zz))
            def _(zz=zz):
                unpack(zz)

    steps(4, 0, 0)
    unpack_part(unpack_q, True)
    steps(2, 1, 3, 1)
    steps(4, 0, 1)
    unpack_part(unpack_o, True)
    steps(3, 1, 2, 0)
    steps(4, 0, 2)
    steps(4, 1, 2, 0)
    unpack_part(unpack_q, False)
    for j in range(4):
        qw[400 * j:400 * j + 400, :] = qf[j].astype(BF16)
    queries[...] = dot(normed[...], qw[...]).astype(BF16)

    for clip in range(2):
        for n in range(1, FRAMES):
            frm = (f + n) % FRAMES
            place = pl.multiple_of(16 * frm, 16)
            got = lat.at[clip, pl.ds(place, 16), :]
            copy(got, got, pool_send.at[clip, frm], pool_recv.at[clip, frm], (dp, frm)).wait_recv()

    kl[...] = dot(lat[...].reshape(256, V), kb[...].reshape(V, HW)).astype(BF16)

    low = lax.broadcasted_iota(jnp.int32, (128, 128), 1) < HD
    scale = HD ** -0.5
    zero = jnp.zeros((128, 128), BF16)

    def split(block):
        return jnp.concatenate([jnp.where(low, block, zero), jnp.where(low, zero, block)], axis=0)

    for clip in range(2):
        rows = slice(TP * clip, TP * clip + TP)
        lats = slice(128 * clip, 128 * clip + 128)
        for p in range(7):
            cols = slice(128 * p, 128 * p + 128)
            scores = dot_nt(split(kl[lats, cols]), queries[rows, cols]).reshape(2, 128, TP) * scale
            top = jnp.max(scores, axis=1, keepdims=True)
            shifted = jnp.exp(scores - top)
            probs_all[7 * clip + p] = shifted / jnp.sum(shifted, axis=1, keepdims=True)

    steps(3, 1, 3, 1)
    steps(4, 0, 3)
    steps(4, 1, 1)
    unpack_part(unpack_o, False)
    for j in range(4):
        ow[224 * j:224 * j + 224, :] = of[j].astype(BF16)
    ga[...] = dot_nt(go[...], ow[...]).astype(BF16)
    steps(4, 1, 3)
    key_w = kb[...].reshape(V, HW)
    value_w = vb[...].reshape(V, HW)
    vl[...] = dot(lat[...].reshape(256, V), value_w).astype(BF16)

    def back_copy(clip, to, frm):
        rows = pl.multiple_of(16 * to, 16)
        return copy(
            back.at[clip, pl.ds(rows, 16), :], grad_pooled.at[2 * frm + clip],
            back_send.at[clip, to], back_recv.at[clip, frm], (dp, to))

    for clip in range(2):
        rows = slice(TP * clip, TP * clip + TP)
        lats = slice(128 * clip, 128 * clip + 128)
        for p in range(7):
            cols = slice(128 * p, 128 * p + 128)
            qp = queries[rows, cols]
            gp = ga[rows, cols]
            kd = split(kl[lats, cols])
            vd = split(vl[lats, cols])
            grad_probs = dot_nt(vd, gp).reshape(2, 128, TP)
            probs = probs_all[7 * clip + p]
            probs_low = probs.astype(BF16)
            row_term = jnp.sum(probs_low.astype(F32) * grad_probs, axis=1, keepdims=True)
            grad_scores = (probs * (grad_probs - row_term) * scale).astype(BF16).reshape(256, TP)
            dk = dot(grad_scores, qp)
            dv = dot(probs_low.reshape(256, TP), gp)
            gk[lats, cols] = jnp.where(low, dk[0:128], dk[128:256]).astype(BF16)
            gv[lats, cols] = jnp.where(low, dv[0:128], dv[128:256]).astype(BF16)
            gq[rows, cols] = dot_tn(grad_scores, kd).astype(BF16)
        result = dot_nt(gk[lats, :], key_w) + dot_nt(gv[lats, :], value_w)
        back[clip] = result.astype(BF16)
        for n in range(1, FRAMES):
            back_copy(clip, (f + n) % FRAMES, f).start()
        mine = pl.multiple_of(16 * f, 16)
        pltpu.make_async_copy(
            back.at[clip, pl.ds(mine, 16), :], grad_pooled.at[2 * f + clip], own_sem.at[clip]
        ).start()

    grad_normed = dot_nt(gq[...], qw[...])
    for clip in range(2):
        rows = slice(TP * clip, TP * clip + TP)
        g = grad_normed[rows] * gain[0:1, :]
        unit_rows = unit[rows, :]
        mean_g = jnp.sum(g, axis=1, keepdims=True) * (1.0 / D)
        mean_gu = jnp.sum(g * unit_rows, axis=1, keepdims=True) * (1.0 / D)
        out = inverses[clip] * (g - mean_g - unit_rows * mean_gu)
        for j in range(13):
            xs[j, pl.ds(clip, TP, stride=2), :] = out[:, 128 * j:128 * j + 128]
    for t in range(TEXT):
        both = jnp.concatenate([xs[j, 2 * t:2 * t + 2, :] for j in range(13)], axis=1)
        grad_text[t] = both[:, 0:D].astype(BF16)

    for moving in sends:
        moving.wait_send()
    for clip in range(2):
        for n in range(1, FRAMES):
            to = (f + n) % FRAMES
            pool_copy(clip, to, f).wait_send()
            back_copy(clip, to, f).wait_send()
        for n in range(1, FRAMES):
            frm = (f + n) % FRAMES
            got = grad_pooled.at[2 * frm + clip]
            copy(got, got, back_send.at[clip, frm], back_recv.at[clip, frm], (dp, frm)).wait_recv()
        mine = pl.multiple_of(16 * f, 16)
        pltpu.make_async_copy(
            back.at[clip, pl.ds(mine, 16), :], grad_pooled.at[2 * f + clip], own_sem.at[clip]
        ).wait()

    @pl.when(at_low)
    def _():
        for w in range(4):
            for k in range(4):
                cross(0, k, w, 4 + k).wait_send()

    @pl.when(at_high)
    def _():
        for w in range(4):
            for k in range(4):
                cross(1, k, w, 3 - k).wait_send()


def settle(text_in, pooled_in, text_out, pooled_out):
    pooled_out[...] = pooled_in[...]
    text_out[...] = text_in[...]


def shards(video, pool_w, text, gain, lengths, cot, q_w, k_w, v_w, o_w):
    vmem = pl.BlockSpec(memory_space=pltpu.VMEM)
    smem = pl.BlockSpec(memory_space=pltpu.SMEM)
    dma = pltpu.SemaphoreType.DMA
    anywhere = pl.BlockSpec(memory_space=pl.ANY)
    grad_text, grad_pooled = pl.pallas_call(
        kernel,
        out_shape=(
            jax.ShapeDtypeStruct((TEXT, 2, D), BF16),
            jax.ShapeDtypeStruct((16, LAT, V), BF16),
        ),
        in_specs=[anywhere, vmem, anywhere, vmem, smem, anywhere, anywhere, anywhere, anywhere, anywhere],
        out_specs=(vmem, anywhere),
        scratch_shapes=[
            pltpu.VMEM((4, 4, 2, 2, 16, QL), BF16),
            pltpu.VMEM((4, 4, 2, 2, 16, OL), BF16),
            pltpu.VMEM((4, 4, 2, 2, 16, HW), BF16),
            pltpu.VMEM((4, 4, 2, 2, 16, HW), BF16),
            pltpu.VMEM((DP, HW), BF16),
            pltpu.VMEM((HW, DP), BF16),
            pltpu.VMEM((4, 400, HW), F32),
            pltpu.VMEM((4, 224, DP), F32),
            pltpu.VMEM((16, QL), F32),
            pltpu.VMEM((16, OL), F32),
            pltpu.VMEM((13, ROWS, 128), F32),
            pltpu.VMEM((13, ROWS, 128), F32),
            pltpu.VMEM((8, DP), F32),
            pltpu.VMEM((ROWS, DP), F32),
            pltpu.VMEM((ROWS, DP), BF16),
            pltpu.VMEM((ROWS, DP), BF16),
            pltpu.VMEM((ROWS, HW), BF16),
            pltpu.VMEM((ROWS, HW), BF16),
            pltpu.VMEM((256, V), BF16),
            pltpu.VMEM((2, 128, V), BF16),
            pltpu.VMEM((256, HW), BF16),
            pltpu.VMEM((256, HW), BF16),
            pltpu.VMEM((256, HW), BF16),
            pltpu.VMEM((256, HW), BF16),
            pltpu.VMEM((ROWS, HW), BF16),
            pltpu.VMEM((2, 128, V), BF16),
            dma((4, 2, 16)),
            dma((4, 2, 16)),
            dma((4, 4)),
            dma((4,)),
            dma((2, FRAMES)),
            dma((2, FRAMES)),
            dma((2, FRAMES)),
            dma((2, FRAMES)),
            dma((2,)),
            dma((7,)),
            pltpu.VMEM((TEXT, 2, D), BF16),
            pltpu.VMEM((TEXT, 2, D), BF16),
            pltpu.VMEM((512, V), BF16),
            pltpu.VMEM((25, HW), BF16),
            pltpu.VMEM((14, D), BF16),
            pltpu.VMEM((14, 2, 128, TP), F32),
        ],
        compiler_params=pltpu.CompilerParams(
            collective_id=0, has_side_effects=True, vmem_limit_bytes=60 * 1024 * 1024
        ),
    )(
        video.reshape(512, V), pool_w.reshape(LAT, 32), text.transpose(1, 0, 2), gain, lengths,
        cot.transpose(1, 0, 2), q_w, k_w, v_w, o_w,
    )
    grad_text, grad_pooled = pl.pallas_call(
        settle,
        out_shape=(
            jax.ShapeDtypeStruct((TEXT, 2, D), BF16),
            jax.ShapeDtypeStruct((16, LAT, V), BF16),
        ),
        in_specs=[vmem, vmem],
        out_specs=(vmem, vmem),
    )(grad_text, grad_pooled)
    return grad_text.transpose(1, 0, 2), grad_pooled


def solution(mesh):
    both = ("dp", "frame")
    return jax.shard_map(
        shards,
        mesh=mesh,
        in_specs=(
            P("dp", "frame", None, None), P("frame", None, None), P(both, None, None), P(), P(both),
            P(both, None, None), P("dp", None), P("dp", None), P("dp", None), P("dp", None),
        ),
        out_specs=(P(both, None, None), P("dp", "frame", None)),
        check_vma=False,
    )
```
